32 devices in a mesh: tx: 4 (over x, core), ty: 8 (over z, y).
Axes of the slice: x: 2, y: 2, z: 4, core: 2. Of those that a mesh axis runs over, the one named last changes fastest.
Arguments:
- prior_state: float32 [2, 32, 256, 256], P(None, 'tx', 'ty'), may hold values from -6 to 6
- east_vel: float32 [2, 32, 256], P(None, 'tx', 'ty'), may hold values from -0.4 to 0.4
- north_vel: float32 [2, 32, 256], P(None, 'tx', 'ty'), may hold values from -0.4 to 0.4
- owner_tiles: int32 [3, 8], replicated, may hold values from 0 to 31, as said below
- obs_cells: int32 [3, 8, 128], replicated, may hold values from 0 to 511
- obs_value: float32 [3, 8, 128], replicated, may hold values from -6 to 6
- obs_error: float32 [3, 8, 128], replicated, may hold values from 0.1 to 1
- obs_pert: float32 [3, 8, 128, 256], replicated, may hold values from -6 to 6
Outputs:
- analysis: float32 [2, 32, 256, 256], P(None, 'tx', 'ty')
The draws below stay inside these ranges and needn't reach their ends.
Inputs may be any that keep to these rules, and one draw needn't show every extreme that they name: `owner_tiles`: the 8 owners of one section hold distinct tiles.
All inputs are finite; a program needn't handle non-finite values.
Results may differ from the reference program's by a relative error of at most 0.0001.
Values sent between devices are 32-bit elements; how exact they have to be, the bound alone decides.
A program may use at most 128 MiB of HBM per device.

```python
import math
import jax
import jax.numpy as jnp
from jax import lax

LEV = 2
CX = 8
CY = 32
MEM = 256
NOBS = 128
NOWN = 8
SECTIONS = 3
NX = 32
NY = 256
NTILES = 32
N_TY = 8


def draw_owner_tiles(key, part):
    section_keys = jax.random.split(key, SECTIONS)
    rows_list = [jax.random.permutation(section_keys[section_num], NTILES)[:NOWN] for section_num in range(SECTIONS)]
    return jnp.stack(rows_list).astype(jnp.int32)


def touch_ends(entries, stream_key, low, largest):
    extent = entries.shape
    place = [jax.random.randint(jax.random.fold_in(stream_key, axis), (), 0, extent[axis]) for axis in range(len(extent))]
    entries = entries.at[tuple(place)].set(low)
    longest = extent.index(max(extent))
    place[longest] = (place[longest] + 1) % extent[longest]
    return entries.at[tuple(place)].set(largest)


def steps_of(own_key, shape, cuts, least, largest):
    factor_of = 1.0
    for position, parts in cuts:
        draws = jax.random.uniform(jax.random.fold_in(jax.random.fold_in(own_key, 6), position), (parts,), jnp.float32, least / len(cuts), largest / len(cuts))
        factor_of = factor_of * jnp.repeat(jnp.exp(draws), shape[position] // parts).reshape((-1,) + (1,) * (len(shape) - 1 - position))
    return factor_of


def noise(own_key, shape, scale, limit, shards=(), held_as=jnp.bfloat16):
    values = scale * jax.random.normal(own_key, shape, jnp.float32)
    if shards:
        values = values * steps_of(own_key, shape, shards, -0.22, 0.18)
    return jnp.clip(values, -limit, limit).astype(held_as)


def setup_inputs(seed: int = 0) -> dict:
    arg_keys = jax.random.split(jax.random.key(seed), 9)
    return {
        "prior_state": noise(arg_keys[0], (LEV, NX, NY, MEM), 1.0, 6.0, ((1, 4), (2, 8)), jnp.float32),
        "east_vel": jnp.clip(jax.random.uniform(arg_keys[1], (LEV, NX, NY), jnp.float32, -0.4, 0.4) * steps_of(arg_keys[1], (LEV, NX, NY), ((1, 4), (2, 8)), -0.4, 0.0), -0.4, 0.4),
        "north_vel": jnp.clip(jax.random.uniform(arg_keys[2], (LEV, NX, NY), jnp.float32, -0.4, 0.4) * steps_of(arg_keys[2], (LEV, NX, NY), ((1, 4), (2, 8)), -0.4, 0.0), -0.4, 0.4),
        "owner_tiles": draw_owner_tiles(jax.random.fold_in(arg_keys[8], 71), 0),
        "obs_cells": touch_ends(jax.random.randint(arg_keys[4], (SECTIONS, NOWN, NOBS), 0, LEV * CX * CY), jax.random.fold_in(arg_keys[4], 1), 0, (LEV * CX * CY) - 1).astype(jnp.int32),
        "obs_value": noise(arg_keys[5], (SECTIONS, NOWN, NOBS), 1.0, 6.0, (), jnp.float32),
        "obs_error": jnp.clip(jnp.exp(jax.random.uniform(arg_keys[6], (SECTIONS, NOWN, NOBS), jnp.float32, math.log(0.1), math.log(1.0))), 0.1, 1.0),
        "obs_pert": noise(arg_keys[7], (SECTIONS, NOWN, NOBS, MEM), 1.0, 6.0, (), jnp.float32),
    }


NU_COEF = 0.2
DAMP_COEF = 0.3
VERT_COEF = 0.6

def advance(prior_state, east_vel, north_vel):
    padded = jnp.pad(prior_state, ((0, 0), (1, 1), (1, 1), (0, 0)))
    east_cells = padded[:, 2:, 1:-1]
    west_cells = padded[:, :-2, 1:-1]
    north_cells = padded[:, 1:-1, 2:]
    south_cells = padded[:, 1:-1, :-2]
    east_speed = east_vel[..., None]
    north_speed = north_vel[..., None]
    return prior_state + NU_COEF * (east_cells + west_cells + north_cells + south_cells - 4.0 * prior_state) - 0.5 * east_speed * (east_cells - west_cells) - 0.5 * north_speed * (north_cells - south_cells) - DAMP_COEF * jnp.tanh(prior_state)

def ramp(distance, radius):
    return jnp.square(jnp.maximum(0.0, 1.0 - jnp.abs(distance) / radius))

def taper(start_x, count_x, start_y, count_y, obs_x, obs_y, obs_level, levels, radius_x, radius_y):
    cell_x = start_x + jnp.arange(count_x, dtype=jnp.int32)
    cell_y = start_y + jnp.arange(count_y, dtype=jnp.int32)
    weight_x = ramp((cell_x[:, None] - obs_x[None, :]).astype(jnp.float32), radius_x)
    weight_y = ramp((cell_y[:, None] - obs_y[None, :]).astype(jnp.float32), radius_y)
    same_level = jnp.arange(levels, dtype=jnp.int32)[:, None] == obs_level[None, :]
    weight_l = jnp.where(same_level, jnp.float32(1.0), jnp.float32(VERT_COEF))
    joined = weight_l[:, None, None, :] * weight_x[None, :, None, :] * weight_y[None, None, :, :]
    return joined.reshape(levels * count_x * count_y, obs_x.shape[0])

def positions(tile_id, obs_cell, size_x, size_y, tiles_y):
    tile_i = tile_id // tiles_y
    tile_j = tile_id % tiles_y
    obs_level = obs_cell // (size_x * size_y)
    remain = obs_cell % (size_x * size_y)
    obs_x = tile_i * size_x + remain // size_y
    obs_y = tile_j * size_y + remain % size_y
    return (obs_level.astype(jnp.int32), obs_x.astype(jnp.int32), obs_y.astype(jnp.int32))

def prepare(prior_obs, values, errors, obs_noise, members):
    ens_mean = lax.optimization_barrier(jnp.mean(prior_obs, axis=1, keepdims=True))
    anomaly = prior_obs - ens_mean
    spread = lax.optimization_barrier(jnp.sum(anomaly * anomaly, axis=1)) / (members - 1)
    factor = 1.0 / ((members - 1) * (spread + errors))
    innovation = values[:, None] + jnp.sqrt(errors)[:, None] * obs_noise - prior_obs
    return (anomaly, innovation, factor)

def update(state_anom, anomaly, innovation, factor, weights_taper):
    covar = jnp.dot(state_anom, anomaly.T, precision=lax.Precision.HIGHEST, preferred_element_type=jnp.float32)
    weights = covar * weights_taper * factor[None, :]
    return jnp.dot(weights, innovation, precision=lax.Precision.HIGHEST, preferred_element_type=jnp.float32)

def reference(prior_state, east_vel, north_vel, owner_tiles, obs_cells, obs_value, obs_error, obs_pert):
    model_state = advance(prior_state, east_vel, north_vel)
    zero_index = jnp.zeros((), jnp.int32)
    for section_num in range(SECTIONS):
        flat_state = model_state.reshape(LEV * NX * NY, MEM)
        state_anom = (flat_state - lax.optimization_barrier(jnp.mean(flat_state, axis=1, keepdims=True))).reshape(LEV, NX, NY, MEM)
        padded = jnp.pad(state_anom, ((0, 0), (3 * CX, 3 * CX), (3 * CY, 3 * CY), (0, 0)))
        total_inc = jnp.zeros(padded.shape, jnp.float32)
        for owner_num in range(NOWN):
            tile_id = owner_tiles[section_num, owner_num]
            obs_level, obs_x, obs_y = positions(tile_id, obs_cells[section_num, owner_num], CX, CY, N_TY)
            glob_index = (obs_level * (NX * NY) + obs_x * NY + obs_y).astype(jnp.int32)
            prior_obs = flat_state[glob_index]
            anomaly, innovation, factor = prepare(prior_obs, obs_value[section_num, owner_num], obs_error[section_num, owner_num], obs_pert[section_num, owner_num], MEM)
            start_x = (tile_id // N_TY * CX).astype(jnp.int32)
            start_y = (tile_id % N_TY * CY).astype(jnp.int32)
            corner = (zero_index, start_x, start_y, zero_index)
            window = lax.dynamic_slice(padded, corner, (LEV, 7 * CX, 7 * CY, MEM)).reshape(LEV * 49 * CX * CY, MEM)
            weights_taper = taper(start_x - 3 * CX, 7 * CX, start_y - 3 * CY, 7 * CY, obs_x, obs_y, obs_level, LEV, 3.0 * CX, 3.0 * CY)
            increment = update(window, anomaly, innovation, factor, weights_taper).reshape(LEV, 7 * CX, 7 * CY, MEM)
            before = lax.dynamic_slice(total_inc, corner, (LEV, 7 * CX, 7 * CY, MEM))
            total_inc = lax.dynamic_update_slice(total_inc, before + increment, corner)
        model_state = model_state + total_inc[:, 3 * CX:3 * CX + NX, 3 * CY:3 * CY + NY]
    return model_state
```

```python
import functools

import jax
import jax.numpy as jnp
from jax import lax
from jax.experimental import pallas as pl
from jax.experimental.pallas import tpu as pltpu
from jax.sharding import PartitionSpec as P

NU_COEF = 0.2
DAMP_COEF = 0.3
VERT_COEF = 0.6


def passed(array, axis, by):
    count = lax.axis_size(axis)
    return lax.ppermute(array, axis, [(i, i + by) for i in range(count) if 0 <= i + by < count])


def advance(prior_state, east_vel, north_vel):
    east_cells = jnp.concatenate([prior_state[:, 1:], passed(prior_state[:, :1], "tx", -1)], axis=1)
    west_cells = jnp.concatenate([passed(prior_state[:, -1:], "tx", 1), prior_state[:, :-1]], axis=1)
    north_cells = jnp.concatenate([prior_state[:, :, 1:], passed(prior_state[:, :, :1], "ty", -1)], axis=2)
    south_cells = jnp.concatenate([passed(prior_state[:, :, -1:], "ty", 1), prior_state[:, :, :-1]], axis=2)
    east_speed = east_vel[..., None]
    north_speed = north_vel[..., None]
    return (
        prior_state
        + NU_COEF * (east_cells + west_cells + north_cells + south_cells - 4.0 * prior_state)
        - 0.5 * east_speed * (east_cells - west_cells)
        - 0.5 * north_speed * (north_cells - south_cells)
        - DAMP_COEF * jnp.tanh(prior_state)
    )


def positions(tile_id, obs_cell, size_x, size_y, tiles_y):
    tile_i = tile_id // tiles_y
    tile_j = tile_id % tiles_y
    obs_level = obs_cell // (size_x * size_y)
    remain = obs_cell % (size_x * size_y)
    obs_x = tile_i * size_x + remain // size_y
    obs_y = tile_j * size_y + remain % size_y
    return (obs_level, obs_x, obs_y)


def spread_kernel(ntx, nty, column_ref, row_ref, mine_ref, out_ref, rows_ref, outgo_ref, income_ref,
                  send_a, recv_a, send_b, recv_b, send_c, recv_c, send_d, recv_d):
    mesh_ids = pl.DeviceIdType.MESH
    i = lax.axis_index("tx")
    j = lax.axis_index("ty")
    sections, owners = 3, column_ref.shape[1]
    sections = column_ref.shape[0]
    halves = owners * 2
    share = halves // ntx
    row_peers = [lax.rem(j + k, nty) for k in range(1, nty)]
    col_peers = [lax.rem(i + k, ntx) for k in range(1, ntx)]
    barrier = pltpu.get_barrier_semaphore()
    for t in row_peers:
        pl.semaphore_signal(barrier, inc=1, device_id=(i, t), device_id_type=mesh_ids)
    for c in col_peers:
        pl.semaphore_signal(barrier, inc=1, device_id=(c, j), device_id_type=mesh_ids)
    pl.semaphore_wait(barrier, nty - 1 + ntx - 1)

    sent = []
    for k, t in enumerate(row_peers):
        copy = pltpu.make_async_remote_copy(
            mine_ref.at[t], rows_ref.at[j], send_a.at[k], recv_a.at[j],
            device_id=(i, t), device_id_type=mesh_ids)
        copy.start()
        sent.append(copy)
    rows_ref[j] = mine_ref[j]
    for k, t in enumerate(row_peers):
        pltpu.make_async_remote_copy(
            mine_ref.at[t], rows_ref.at[t], send_a.at[k], recv_a.at[t],
            device_id=(i, t), device_id_type=mesh_ids).wait_recv()

    for s in range(sections):
        for o in range(owners):
            here = column_ref[s, o] == i
            for half in range(2):
                h = 2 * o + half
                outgo_ref[h // share, h % share, s] = jnp.where(here, rows_ref[row_ref[s, o], s, half], 0.0)
    for k, c in enumerate(col_peers):
        copy = pltpu.make_async_remote_copy(
            outgo_ref.at[c], income_ref.at[i], send_b.at[k], recv_b.at[i],
            device_id=(c, j), device_id_type=mesh_ids)
        copy.start()
        sent.append(copy)
    total = outgo_ref[i]
    for k, c in enumerate(col_peers):
        pltpu.make_async_remote_copy(
            outgo_ref.at[c], income_ref.at[c], send_b.at[k], recv_b.at[c],
            device_id=(c, j), device_id_type=mesh_ids).wait_recv()
        total = total + income_ref[c]
    out_ref[i, j] = total

    for k, t in enumerate(row_peers):
        copy = pltpu.make_async_remote_copy(
            out_ref.at[i, j], out_ref.at[i, j], send_c.at[k], recv_c.at[j],
            device_id=(i, t), device_id_type=mesh_ids)
        copy.start()
        sent.append(copy)
    for k, t in enumerate(row_peers):
        pltpu.make_async_remote_copy(
            out_ref.at[i, t], out_ref.at[i, t], send_c.at[k], recv_c.at[t],
            device_id=(i, t), device_id_type=mesh_ids).wait_recv()

    held = [i]
    count = 0
    bit = ntx // 2
    while bit >= 1:
        def flip(b, bit=bit):
            return b + bit - 2 * bit * lax.rem(b // bit, 2)
        partner = flip(i)
        for b in held:
            copy = pltpu.make_async_remote_copy(
                out_ref.at[b], out_ref.at[b], send_d.at[count], recv_d.at[b],
                device_id=(partner, j), device_id_type=mesh_ids)
            copy.start()
            sent.append(copy)
            count += 1
        fresh = [flip(b) for b in held]
        for b in fresh:
            pltpu.make_async_remote_copy(
                out_ref.at[b], out_ref.at[b], send_d.at[0], recv_d.at[b],
                device_id=(partner, j), device_id_type=mesh_ids).wait_recv()
        held = held + fresh
        bit //= 2
    for copy in sent:
        copy.wait_send()


def spread(payload, owner_tiles, ntx, nty):
    sections, count, members = payload.shape
    owners = owner_tiles.shape[1]
    rows, lanes, share = count // nty, members // 2, owners * 2 // ntx
    mine = payload.reshape(sections, nty, rows, 2, lanes).transpose(1, 0, 3, 2, 4)
    dma = pltpu.SemaphoreType.DMA
    everything = pl.pallas_call(
        functools.partial(spread_kernel, ntx, nty),
        out_shape=jax.ShapeDtypeStruct((ntx, nty, share, sections, rows, lanes), jnp.float32),
        in_specs=[pl.BlockSpec(memory_space=pltpu.SMEM)] * 2 + [pl.BlockSpec(memory_space=pltpu.VMEM)],
        out_specs=pl.BlockSpec(memory_space=pltpu.VMEM),
        scratch_shapes=[
            pltpu.VMEM((nty, sections, 2, rows, lanes), jnp.float32),
            pltpu.VMEM((ntx, share, sections, rows, lanes), jnp.float32),
            pltpu.VMEM((ntx, share, sections, rows, lanes), jnp.float32),
            dma((nty,)), dma((nty,)), dma((ntx,)), dma((ntx,)),
            dma((nty,)), dma((nty,)), dma((ntx,)), dma((ntx,)),
        ],
        compiler_params=pltpu.CompilerParams(
            collective_id=0, has_side_effects=True, vmem_limit_bytes=24 * 2**20),
    )(owner_tiles // nty, owner_tiles % nty, mine)
    return everything


def terms(a):
    high = a.astype(jnp.bfloat16)
    return high, (a - high.astype(jnp.float32)).astype(jnp.bfloat16)


def update_kernel(chunk, reach_x, reach_y, state_ref, slots_ref, noise_ref, column_ref, line_ref, out_ref,
                  all_ref, anom_ref, innov_ref):
    ntx, nty, share, sections, rows, lanes = slots_ref.shape
    cells, members = state_ref.shape
    observed = noise_ref.shape[1]
    per = nty * rows
    for s in range(sections):
        for h in range(2 * observed // per):
            all_ref[pl.ds(s * observed + h // 2 * per, per), pl.ds(h % 2 * lanes, lanes)] = slots_ref[
                h // share, :, h % share, s].reshape(per, lanes)
    total = sections * observed + cells
    all_ref[pl.ds(sections * observed, cells), :] = state_ref[...]
    for s in range(sections):
        start = s * observed
        prior_obs = all_ref[pl.ds(start, observed), :]
        anomaly = prior_obs - jnp.mean(prior_obs, axis=1, keepdims=True)
        value = column_ref[pl.ds(start, observed), 3:4]
        error = column_ref[pl.ds(start, observed), 4:5]
        factor = 1.0 / (jnp.sum(anomaly * anomaly, axis=1, keepdims=True) + (members - 1) * error)
        innovation = (value + jnp.sqrt(error) * noise_ref[s] - prior_obs) * factor
        high, low = terms(anomaly)
        anom_ref[...] = jnp.concatenate([high, high, low], axis=1)
        high, low = terms(innovation)
        innov_ref[...] = jnp.concatenate([high, high, low], axis=0)
        level_o = line_ref[s, 0:1, :]
        x_o = line_ref[s, 1:2, :]
        y_o = line_ref[s, 2:3, :]

        def refresh(at):
            block = all_ref[pl.ds(at, chunk), :]
            level = column_ref[pl.ds(at, chunk), 0:1]
            x = column_ref[pl.ds(at, chunk), 1:2]
            y = column_ref[pl.ds(at, chunk), 2:3]
            high, low = terms(block - jnp.mean(block, axis=1, keepdims=True))
            covar = lax.dot_general(
                jnp.concatenate([high, low, high], axis=1), anom_ref[...], (((1,), (1,)), ((), ())),
                preferred_element_type=jnp.float32)
            near_x = jnp.maximum(0.0, 1.0 - jnp.abs(x - x_o) * (1.0 / reach_x))
            near_y = jnp.maximum(0.0, 1.0 - jnp.abs(y - y_o) * (1.0 / reach_y))
            near = near_x * near_y
            weights = covar * (near * near * jnp.where(level == level_o, 1.0, VERT_COEF))
            high, low = terms(weights)
            return block + jnp.dot(
                jnp.concatenate([high, low, high], axis=1), innov_ref[...], preferred_element_type=jnp.float32)

        first = start + observed
        if s + 1 < sections:
            @pl.loop(0, (total - first) // chunk)
            def _(n):
                at = pl.multiple_of(first + n * chunk, chunk)
                all_ref[pl.ds(at, chunk), :] = refresh(at)
        else:
            for n in range(cells // chunk):
                out_ref[pl.ds(n * chunk, chunk), :] = refresh(first + n * chunk)


def update(state, slots, noise, column, line, reach_x, reach_y):
    sections, observed, members = noise.shape
    cells = state.shape[0]
    total = sections * observed + cells
    chunk = 256
    whole = pl.BlockSpec(memory_space=pltpu.VMEM)
    return pl.pallas_call(
        functools.partial(update_kernel, chunk, reach_x, reach_y),
        out_shape=jax.ShapeDtypeStruct((cells, members), jnp.float32),
        in_specs=[whole] * 5,
        out_specs=whole,
        scratch_shapes=[
            pltpu.VMEM((total, members), jnp.float32),
            pltpu.VMEM((observed, 3 * members), jnp.bfloat16),
            pltpu.VMEM((3 * observed, members), jnp.bfloat16),
        ],
        compiler_params=pltpu.CompilerParams(vmem_limit_bytes=48 * 2**20),
    )(state, slots, noise, column, line)


def on_device(
    prior_state, east_vel, north_vel, owner_tiles, obs_cells, obs_value, obs_error, obs_pert
):
    levels, size_x, size_y, members = prior_state.shape
    section_count, owner_count, obs_count = obs_cells.shape
    ntx, nty = lax.axis_size("tx"), lax.axis_size("ty")
    column_idx = lax.axis_index("tx")
    row_idx = lax.axis_index("ty")
    my_tile = column_idx * nty + row_idx
    cells = levels * size_x * size_y
    state = advance(prior_state, east_vel, north_vel).reshape(cells, members)

    mine = owner_tiles == my_tile
    my_cells = jnp.sum(jnp.where(mine[:, :, None], obs_cells, 0), axis=1)
    chosen = (my_cells.reshape(-1)[:, None] == jnp.arange(cells)[None, :]).astype(jnp.float32)
    payload = jnp.dot(chosen, state, precision=lax.Precision.HIGHEST)
    slots = spread(payload.reshape(section_count, obs_count, members), owner_tiles, ntx, nty)

    level_o, x_o, y_o = positions(owner_tiles[:, :, None], obs_cells, size_x, size_y, nty)
    own = jnp.arange(cells, dtype=jnp.int32)
    level_c = own // (size_x * size_y)
    x_c = column_idx * size_x + own % (size_x * size_y) // size_y
    y_c = row_idx * size_y + own % size_y
    zero = jnp.zeros((cells,), jnp.float32)
    column = jnp.stack([
        jnp.concatenate([a.reshape(-1).astype(jnp.float32), b.astype(jnp.float32)])
        for a, b in ((level_o, level_c), (x_o, x_c), (y_o, y_c), (obs_value, zero), (obs_error, zero))
    ], axis=1)
    line = jnp.stack([a.reshape(section_count, -1).astype(jnp.float32) for a in (level_o, x_o, y_o)], axis=1)
    noise = obs_pert.reshape(section_count, owner_count * obs_count, members)
    out = update(state, slots, noise, column, line, 3.0 * size_x, 3.0 * size_y)
    return out.reshape(levels, size_x, size_y, members)


def solution(mesh):
    placed = (
        P(None, "tx", "ty", None),
        P(None, "tx", "ty"),
        P(None, "tx", "ty"),
        P(),
        P(),
        P(),
        P(),
        P(),
    )
    return jax.shard_map(
        on_device, mesh=mesh, in_specs=placed, out_specs=P(None, "tx", "ty", None), check_vma=False
    )
```

```python
import functools

import jax
import jax.numpy as jnp
from jax import lax
from jax.experimental import pallas as pl
from jax.experimental.pallas import tpu as pltpu
from jax.sharding import PartitionSpec as P

NU_COEF = 0.2
DAMP_COEF = 0.3
VERT_COEF = 0.6


def positions(tile_id, obs_cell, size_x, size_y, tiles_y):
    tile_i = tile_id // tiles_y
    tile_j = tile_id % tiles_y
    obs_level = obs_cell // (size_x * size_y)
    remain = obs_cell % (size_x * size_y)
    obs_x = tile_i * size_x + remain // size_y
    obs_y = tile_j * size_y + remain % size_y
    return (obs_level, obs_x, obs_y)


def spread_kernel(ntx, nty, column_ref, row_ref, prior_ref, speed_ref, mycell_ref, state_ref, out_ref,
                  pad_ref, edge_ref, halo_x_ref, halo_y_ref, mine_ref, rows_refs, outgo_ref, income_ref,
                  send_h, recv_h, send_a, recv_a, send_b, recv_b, send_c, recv_c, send_d, recv_d):
    mesh_ids = pl.DeviceIdType.MESH
    i = lax.axis_index("tx")
    j = lax.axis_index("ty")
    levels, size_x, size_y, members = prior_ref.shape
    cells = levels * size_x * size_y
    sections, owners = column_ref.shape
    share, rows, lanes = out_ref.shape[3:]
    row_peers = [lax.rem(j + k, nty) for k in range(1, nty)]
    col_peers = [lax.rem(i + k, ntx) for k in range(1, ntx)]
    barrier = pltpu.get_barrier_semaphore()
    for t in row_peers:
        pl.semaphore_signal(barrier, inc=1, device_id=(i, t), device_id_type=mesh_ids)
    for c in col_peers:
        pl.semaphore_signal(barrier, inc=1, device_id=(c, j), device_id_type=mesh_ids)
    for lev in range(levels):
        for x in range(size_x):
            edge_ref[0, lev, x:x + 1, :] = prior_ref[lev, x, size_y - 1:size_y, :]
            edge_ref[1, lev, x:x + 1, :] = prior_ref[lev, x, 0:1, :]
    pl.semaphore_wait(barrier, nty - 1 + ntx - 1)

    def sending(src, dst, send_sem, recv_sem, to):
        copy = pltpu.make_async_remote_copy(src, dst, send_sem, recv_sem, device_id=to, device_id_type=mesh_ids)
        copy.start()
        sent.append(copy)

    def arrived(ref, send_sem, recv_sem, to):
        pltpu.make_async_remote_copy(
            ref, ref, send_sem, recv_sem, device_id=to, device_id_type=mesh_ids).wait_recv()

    sent = []
    east, west = (lax.rem(i + 1, ntx), j), (lax.rem(i + ntx - 1, ntx), j)
    north, south = (i, lax.rem(j + 1, nty)), (i, lax.rem(j + nty - 1, nty))
    sending(prior_ref.at[:, size_x - 1], halo_x_ref.at[0], send_h.at[0], recv_h.at[0], east)
    sending(prior_ref.at[:, 0], halo_x_ref.at[1], send_h.at[1], recv_h.at[1], west)
    sending(edge_ref.at[0], halo_y_ref.at[0], send_h.at[2], recv_h.at[2], north)
    sending(edge_ref.at[1], halo_y_ref.at[1], send_h.at[3], recv_h.at[3], south)
    prior = prior_ref[...]
    pad_ref[:, :, 8:8 + size_y, :] = prior
    arrived(halo_x_ref.at[0], send_h.at[0], recv_h.at[0], west)
    arrived(halo_x_ref.at[1], send_h.at[1], recv_h.at[1], east)
    arrived(halo_y_ref.at[0], send_h.at[2], recv_h.at[2], south)
    arrived(halo_y_ref.at[1], send_h.at[3], recv_h.at[3], north)
    for lev in range(levels):
        for x in range(size_x):
            pad_ref[lev, x, 7:8, :] = jnp.where(j == 0, 0.0, halo_y_ref[0, lev, x:x + 1, :])
            pad_ref[lev, x, 8 + size_y:9 + size_y, :] = jnp.where(
                j == nty - 1, 0.0, halo_y_ref[1, lev, x:x + 1, :])
    west_halo = jnp.where(i == 0, 0.0, halo_x_ref[0])[:, None]
    east_halo = jnp.where(i == ntx - 1, 0.0, halo_x_ref[1])[:, None]
    flat = lambda a: a.reshape(cells, members)
    east_cells = flat(jnp.concatenate([prior[:, 1:], east_halo], axis=1))
    west_cells = flat(jnp.concatenate([west_halo, prior[:, :-1]], axis=1))
    north_cells = flat(pad_ref[:, :, 9:9 + size_y, :])
    south_cells = flat(pad_ref[:, :, 7:7 + size_y, :])
    prior = flat(prior)
    state_ref[...] = (
        prior
        + NU_COEF * (east_cells + west_cells + north_cells + south_cells - 4.0 * prior)
        - 0.5 * speed_ref[:, 0:1] * (east_cells - west_cells)
        - 0.5 * speed_ref[:, 1:2] * (north_cells - south_cells)
        - DAMP_COEF * jnp.tanh(prior)
    )
    count = nty * rows
    for s in range(sections):
        places = lax.broadcasted_iota(jnp.int32, (count, cells), 1)
        chosen = jnp.where(mycell_ref[s * count:(s + 1) * count, :] == places, 1.0, 0.0)
        payload = jnp.dot(
            chosen, state_ref[...], precision=lax.Precision.HIGHEST, preferred_element_type=jnp.float32)
        for half in range(2):
            mine_ref[s, :, half] = payload[:, half * lanes:(half + 1) * lanes].reshape(nty, rows, lanes)
        for k, t in enumerate(row_peers):
            sending(mine_ref.at[s, t], rows_refs[s].at[j], send_a.at[s, k], recv_a.at[s, j], (i, t))
        rows_refs[s][j] = mine_ref[s, j]

    for s in range(sections):
        for k, t in enumerate(row_peers):
            arrived(rows_refs[s].at[t], send_a.at[s, k], recv_a.at[s, t], (i, t))
        for o in range(owners):
            here = column_ref[s, o] == i
            for half in range(2):
                h = 2 * o + half
                outgo_ref[s, h // share, h % share] = jnp.where(here, rows_refs[s][row_ref[s, o], half], 0.0)
        for k, c in enumerate(col_peers):
            sending(outgo_ref.at[s, c], income_ref.at[s, i], send_b.at[s, k], recv_b.at[s, i], (c, j))

    for s in range(sections):
        total = outgo_ref[s, i]
        for k, c in enumerate(col_peers):
            arrived(income_ref.at[s, c], send_b.at[s, k], recv_b.at[s, c], (c, j))
            total = total + income_ref[s, c]
        out_ref[s, i, j] = total
        for k, t in enumerate(row_peers):
            sending(out_ref.at[s, i, j], out_ref.at[s, i, j], send_c.at[s, k], recv_c.at[s, j], (i, t))

    def flip(b, bit):
        return b + bit - 2 * bit * lax.rem(b // bit, 2)

    stages = []
    held = [i]
    bit = ntx // 2
    while bit >= 1:
        stages.append((bit, held))
        held = held + [flip(b, bit) for b in held]
        bit //= 2
    for number, (bit, held) in enumerate(stages):
        partner = (flip(i, bit), j)
        for s in range(sections):
            if number == 0:
                for k, t in enumerate(row_peers):
                    arrived(out_ref.at[s, i, t], send_c.at[s, k], recv_c.at[s, t], (i, t))
            else:
                before, had = stages[number - 1]
                for b in had:
                    b = flip(b, before)
                    arrived(out_ref.at[s, b], send_d.at[s, 0], recv_d.at[s, b], partner)
            for n, b in enumerate(held):
                sending(out_ref.at[s, b], out_ref.at[s, b], send_d.at[s, len(held) - 1 + n], recv_d.at[s, b], partner)
    bit, held = stages[-1]
    for s in range(sections):
        for b in held:
            b = flip(b, bit)
            arrived(out_ref.at[s, b], send_d.at[s, 0], recv_d.at[s, b], (flip(i, bit), j))
    for copy in sent:
        copy.wait_send()


def spread(prior_state, speeds, my_cells, owner_tiles, ntx, nty):
    levels, size_x, size_y, members = prior_state.shape
    sections, owners = owner_tiles.shape
    count = my_cells.shape[0] // sections
    rows, lanes, share = count // nty, members // 2, owners * 2 // ntx
    dma = pltpu.SemaphoreType.DMA
    f32 = jnp.float32
    whole = pl.BlockSpec(memory_space=pltpu.VMEM)
    return pl.pallas_call(
        functools.partial(spread_kernel, ntx, nty),
        out_shape=(
            jax.ShapeDtypeStruct((levels * size_x * size_y, members), f32),
            jax.ShapeDtypeStruct((sections, ntx, nty, share, rows, lanes), f32),
        ),
        in_specs=[pl.BlockSpec(memory_space=pltpu.SMEM)] * 2 + [whole] * 3,
        out_specs=(whole, whole),
        scratch_shapes=[
            pltpu.VMEM((levels, size_x, size_y + 16, members), f32),
            pltpu.VMEM((2, levels, size_x, members), f32),
            pltpu.VMEM((2, levels, size_y, members), f32),
            pltpu.VMEM((2, levels, size_x, members), f32),
            pltpu.VMEM((sections, nty, 2, rows, lanes), f32),
            [pltpu.VMEM((nty, 2, rows, lanes), f32)] * sections,
            pltpu.VMEM((sections, ntx, share, rows, lanes), f32),
            pltpu.VMEM((sections, ntx, share, rows, lanes), f32),
            dma((4,)), dma((4,)),
            dma((sections, nty)), dma((sections, nty)), dma((sections, ntx)), dma((sections, ntx)),
            dma((sections, nty)), dma((sections, nty)), dma((sections, ntx)), dma((sections, ntx)),
        ],
        compiler_params=pltpu.CompilerParams(
            collective_id=0, has_side_effects=True, vmem_limit_bytes=32 * 2**20),
    )(owner_tiles // nty, owner_tiles % nty, prior_state, speeds, my_cells)


def terms(a):
    high = a.astype(jnp.bfloat16)
    return high, (a - high.astype(jnp.float32)).astype(jnp.bfloat16)


def update_kernel(chunk, reach_x, reach_y, state_ref, slots_ref, noise_ref, column_ref, line_ref, out_ref,
                  all_ref, anom_ref, innov_ref):
    sections, ntx, nty, share, rows, lanes = slots_ref.shape
    cells, members = state_ref.shape
    observed = noise_ref.shape[1]
    per = nty * rows
    for s in range(sections):
        for h in range(2 * observed // per):
            all_ref[pl.ds(s * observed + h // 2 * per, per), pl.ds(h % 2 * lanes, lanes)] = slots_ref[
                s, h // share, :, h % share].reshape(per, lanes)
    total = sections * observed + cells
    all_ref[pl.ds(sections * observed, cells), :] = state_ref[...]
    for s in range(sections):
        start = s * observed
        prior_obs = all_ref[pl.ds(start, observed), :]
        anomaly = prior_obs - jnp.mean(prior_obs, axis=1, keepdims=True)
        value = column_ref[pl.ds(start, observed), 3:4]
        error = column_ref[pl.ds(start, observed), 4:5]
        factor = 1.0 / (jnp.sum(anomaly * anomaly, axis=1, keepdims=True) + (members - 1) * error)
        innovation = (value + jnp.sqrt(error) * noise_ref[s] - prior_obs) * factor
        high, low = terms(anomaly)
        anom_ref[...] = jnp.concatenate([high, high, low], axis=1)
        high, low = terms(innovation)
        innov_ref[...] = jnp.concatenate([high, high, low], axis=0)
        level_o = line_ref[s, 0:1, :]
        x_o = line_ref[s, 1:2, :]
        y_o = line_ref[s, 2:3, :]

        def refresh(at):
            block = all_ref[pl.ds(at, chunk), :]
            level = column_ref[pl.ds(at, chunk), 0:1]
            x = column_ref[pl.ds(at, chunk), 1:2]
            y = column_ref[pl.ds(at, chunk), 2:3]
            high, low = terms(block - jnp.mean(block, axis=1, keepdims=True))
            covar = lax.dot_general(
                jnp.concatenate([high, low, high], axis=1), anom_ref[...], (((1,), (1,)), ((), ())),
                preferred_element_type=jnp.float32)
            near_x = jnp.maximum(0.0, 1.0 - jnp.abs(x - x_o) * (1.0 / reach_x))
            near_y = jnp.maximum(0.0, 1.0 - jnp.abs(y - y_o) * (1.0 / reach_y))
            near = near_x * near_y
            weights = covar * (near * near * jnp.where(level == level_o, 1.0, VERT_COEF))
            high, low = terms(weights)
            return block + jnp.dot(
                jnp.concatenate([high, low, high], axis=1), innov_ref[...], preferred_element_type=jnp.float32)

        first = start + observed
        if s + 1 < sections:
            @pl.loop(0, (total - first) // chunk)
            def _(n):
                at = pl.multiple_of(first + n * chunk, chunk)
                all_ref[pl.ds(at, chunk), :] = refresh(at)
        else:
            for n in range(cells // chunk):
                out_ref[pl.ds(n * chunk, chunk), :] = refresh(first + n * chunk)


def update(state, slots, noise, column, line, reach_x, reach_y):
    sections, observed, members = noise.shape
    cells = state.shape[0]
    total = sections * observed + cells
    chunk = 256
    whole = pl.BlockSpec(memory_space=pltpu.VMEM)
    return pl.pallas_call(
        functools.partial(update_kernel, chunk, reach_x, reach_y),
        out_shape=jax.ShapeDtypeStruct((cells, members), jnp.float32),
        in_specs=[whole] * 5,
        out_specs=whole,
        scratch_shapes=[
            pltpu.VMEM((total, members), jnp.float32),
            pltpu.VMEM((observed, 3 * members), jnp.bfloat16),
            pltpu.VMEM((3 * observed, members), jnp.bfloat16),
        ],
        compiler_params=pltpu.CompilerParams(vmem_limit_bytes=48 * 2**20),
    )(state, slots, noise, column, line)


def on_device(
    prior_state, east_vel, north_vel, owner_tiles, obs_cells, obs_value, obs_error, obs_pert
):
    levels, size_x, size_y, members = prior_state.shape
    section_count, owner_count, obs_count = obs_cells.shape
    ntx, nty = lax.axis_size("tx"), lax.axis_size("ty")
    column_idx = lax.axis_index("tx")
    row_idx = lax.axis_index("ty")
    my_tile = column_idx * nty + row_idx
    cells = levels * size_x * size_y

    mine = owner_tiles == my_tile
    my_cells = jnp.sum(jnp.where(mine[:, :, None], obs_cells, 0), axis=1)
    speeds = jnp.stack([east_vel.reshape(cells), north_vel.reshape(cells)], axis=1)
    state, slots = spread(prior_state, speeds, my_cells.reshape(-1, 1), owner_tiles, ntx, nty)

    level_o, x_o, y_o = positions(owner_tiles[:, :, None], obs_cells, size_x, size_y, nty)
    own = jnp.arange(cells, dtype=jnp.int32)
    level_c = own // (size_x * size_y)
    x_c = column_idx * size_x + own % (size_x * size_y) // size_y
    y_c = row_idx * size_y + own % size_y
    zero = jnp.zeros((cells,), jnp.float32)
    column = jnp.stack([
        jnp.concatenate([a.reshape(-1).astype(jnp.float32), b.astype(jnp.float32)])
        for a, b in ((level_o, level_c), (x_o, x_c), (y_o, y_c), (obs_value, zero), (obs_error, zero))
    ], axis=1)
    line = jnp.stack([a.reshape(section_count, -1).astype(jnp.float32) for a in (level_o, x_o, y_o)], axis=1)
    noise = obs_pert.reshape(section_count, owner_count * obs_count, members)
    out = update(state, slots, noise, column, line, 3.0 * size_x, 3.0 * size_y)
    return out.reshape(levels, size_x, size_y, members)


def solution(mesh):
    placed = (
        P(None, "tx", "ty", None),
        P(None, "tx", "ty"),
        P(None, "tx", "ty"),
        P(),
        P(),
        P(),
        P(),
        P(),
    )
    return jax.shard_map(
        on_device, mesh=mesh, in_specs=placed, out_specs=P(None, "tx", "ty", None), check_vma=False
    )
```

```python
import functools

import jax
import jax.numpy as jnp
from jax import lax
from jax.experimental import pallas as pl
from jax.experimental.pallas import tpu as pltpu
from jax.sharding import PartitionSpec as P

NU_COEF = 0.2
DAMP_COEF = 0.3
VERT_COEF = 0.6


def positions(tile_id, obs_cell, size_x, size_y, tiles_y):
    tile_i = tile_id // tiles_y
    tile_j = tile_id % tiles_y
    obs_level = obs_cell // (size_x * size_y)
    remain = obs_cell % (size_x * size_y)
    obs_x = tile_i * size_x + remain // size_y
    obs_y = tile_j * size_y + remain % size_y
    return (obs_level, obs_x, obs_y)


def spread_kernel(ntx, nty, column_ref, row_ref, prior_ref, speed_ref, mycell_ref, state_ref, out_ref,
                  pad_ref, edge_ref, halo_x_ref, halo_y_ref, mine_ref, rows_refs, outgo_ref, income_ref,
                  send_h, recv_h, send_a, recv_a, send_b, recv_b, send_c, recv_c, send_d, recv_d):
    mesh_ids = pl.DeviceIdType.MESH
    i = lax.axis_index("tx")
    j = lax.axis_index("ty")
    levels, size_x, size_y, members = prior_ref.shape
    cells = levels * size_x * size_y
    sections, owners = column_ref.shape
    share, rows, lanes = out_ref.shape[3:]
    row_peers = [lax.rem(j + k, nty) for k in range(1, nty)]
    col_peers = [lax.rem(i + k, ntx) for k in range(1, ntx)]
    barrier = pltpu.get_barrier_semaphore()
    for t in row_peers:
        pl.semaphore_signal(barrier, inc=1, device_id=(i, t), device_id_type=mesh_ids)
    for c in col_peers:
        pl.semaphore_signal(barrier, inc=1, device_id=(c, j), device_id_type=mesh_ids)
    for lev in range(levels):
        for x in range(size_x):
            edge_ref[0, lev, x:x + 1, :] = prior_ref[lev, x, size_y - 1:size_y, :]
            edge_ref[1, lev, x:x + 1, :] = prior_ref[lev, x, 0:1, :]
    pl.semaphore_wait(barrier, nty - 1 + ntx - 1)

    def sending(src, dst, send_sem, recv_sem, to):
        copy = pltpu.make_async_remote_copy(src, dst, send_sem, recv_sem, device_id=to, device_id_type=mesh_ids)
        copy.start()
        sent.append(copy)

    def arrived(ref, send_sem, recv_sem, to):
        pltpu.make_async_remote_copy(
            ref, ref, send_sem, recv_sem, device_id=to, device_id_type=mesh_ids).wait_recv()

    sent = []
    east, west = (lax.rem(i + 1, ntx), j), (lax.rem(i + ntx - 1, ntx), j)
    north, south = (i, lax.rem(j + 1, nty)), (i, lax.rem(j + nty - 1, nty))
    sending(prior_ref.at[:, size_x - 1], halo_x_ref.at[0], send_h.at[0], recv_h.at[0], east)
    sending(prior_ref.at[:, 0], halo_x_ref.at[1], send_h.at[1], recv_h.at[1], west)
    sending(edge_ref.at[0], halo_y_ref.at[0], send_h.at[2], recv_h.at[2], north)
    sending(edge_ref.at[1], halo_y_ref.at[1], send_h.at[3], recv_h.at[3], south)
    prior = prior_ref[...]
    pad_ref[:, :, 8:8 + size_y, :] = prior
    arrived(halo_x_ref.at[0], send_h.at[0], recv_h.at[0], west)
    arrived(halo_x_ref.at[1], send_h.at[1], recv_h.at[1], east)
    arrived(halo_y_ref.at[0], send_h.at[2], recv_h.at[2], south)
    arrived(halo_y_ref.at[1], send_h.at[3], recv_h.at[3], north)
    for lev in range(levels):
        for x in range(size_x):
            pad_ref[lev, x, 7:8, :] = jnp.where(j == 0, 0.0, halo_y_ref[0, lev, x:x + 1, :])
            pad_ref[lev, x, 8 + size_y:9 + size_y, :] = jnp.where(
                j == nty - 1, 0.0, halo_y_ref[1, lev, x:x + 1, :])
    west_halo = jnp.where(i == 0, 0.0, halo_x_ref[0])[:, None]
    east_halo = jnp.where(i == ntx - 1, 0.0, halo_x_ref[1])[:, None]
    flat = lambda a: a.reshape(cells, members)
    east_cells = flat(jnp.concatenate([prior[:, 1:], east_halo], axis=1))
    west_cells = flat(jnp.concatenate([west_halo, prior[:, :-1]], axis=1))
    north_cells = flat(pad_ref[:, :, 9:9 + size_y, :])
    south_cells = flat(pad_ref[:, :, 7:7 + size_y, :])
    prior = flat(prior)
    state_ref[...] = (
        prior
        + NU_COEF * (east_cells + west_cells + north_cells + south_cells - 4.0 * prior)
        - 0.5 * speed_ref[:, 0:1] * (east_cells - west_cells)
        - 0.5 * speed_ref[:, 1:2] * (north_cells - south_cells)
        - DAMP_COEF * jnp.tanh(prior)
    )
    count = nty * rows
    for s in range(sections):
        places = lax.broadcasted_iota(jnp.int32, (count, cells), 1)
        chosen = jnp.where(mycell_ref[s * count:(s + 1) * count, :] == places, 1.0, 0.0)
        payload = jnp.dot(
            chosen, state_ref[...], precision=lax.Precision.HIGHEST, preferred_element_type=jnp.float32)
        for half in range(2):
            mine_ref[s, :, half] = payload[:, half * lanes:(half + 1) * lanes].reshape(nty, rows, lanes)
        for k, t in enumerate(row_peers):
            sending(mine_ref.at[s, t], rows_refs[s].at[j], send_a.at[s, k], recv_a.at[s, j], (i, t))
        rows_refs[s][j] = mine_ref[s, j]

    for s in range(sections):
        for k, t in enumerate(row_peers):
            arrived(rows_refs[s].at[t], send_a.at[s, k], recv_a.at[s, t], (i, t))
        for o in range(owners):
            here = column_ref[s, o] == i
            for half in range(2):
                h = 2 * o + half
                outgo_ref[s, h // share, h % share] = jnp.where(here, rows_refs[s][row_ref[s, o], half], 0.0)
        for k, c in enumerate(col_peers):
            sending(outgo_ref.at[s, c], income_ref.at[s, i], send_b.at[s, k], recv_b.at[s, i], (c, j))

    for s in range(sections):
        total = outgo_ref[s, i]
        for k, c in enumerate(col_peers):
            arrived(income_ref.at[s, c], send_b.at[s, k], recv_b.at[s, c], (c, j))
            total = total + income_ref[s, c]
        out_ref[s, i, j] = total
        for k, t in enumerate(row_peers):
            sending(out_ref.at[s, i, j], out_ref.at[s, i, j], send_c.at[s, k], recv_c.at[s, j], (i, t))

    def flip(b, bit):
        return b + bit - 2 * bit * lax.rem(b // bit, 2)

    stages = []
    held = [i]
    bit = ntx // 2
    while bit >= 1:
        stages.append((bit, held))
        held = held + [flip(b, bit) for b in held]
        bit //= 2
    for number, (bit, held) in enumerate(stages):
        partner = (flip(i, bit), j)
        for s in range(sections):
            if number == 0:
                for k, t in enumerate(row_peers):
                    arrived(out_ref.at[s, i, t], send_c.at[s, k], recv_c.at[s, t], (i, t))
            else:
                before, had = stages[number - 1]
                for b in had:
                    b = flip(b, before)
                    arrived(out_ref.at[s, b], send_d.at[s, 0], recv_d.at[s, b], partner)
            for n, b in enumerate(held):
                sending(out_ref.at[s, b], out_ref.at[s, b], send_d.at[s, len(held) - 1 + n], recv_d.at[s, b], partner)
    bit, held = stages[-1]
    for s in range(sections):
        for b in held:
            b = flip(b, bit)
            arrived(out_ref.at[s, b], send_d.at[s, 0], recv_d.at[s, b], (flip(i, bit), j))
    for copy in sent:
        copy.wait_send()


def spread(prior_state, speeds, my_cells, owner_tiles, ntx, nty):
    levels, size_x, size_y, members = prior_state.shape
    sections, owners = owner_tiles.shape
    count = my_cells.shape[0] // sections
    rows, lanes, share = count // nty, members // 2, owners * 2 // ntx
    dma = pltpu.SemaphoreType.DMA
    f32 = jnp.float32
    whole = pl.BlockSpec(memory_space=pltpu.VMEM)
    return pl.pallas_call(
        functools.partial(spread_kernel, ntx, nty),
        out_shape=(
            jax.ShapeDtypeStruct((levels * size_x * size_y, members), f32),
            jax.ShapeDtypeStruct((sections, ntx, nty, share, rows, lanes), f32),
        ),
        in_specs=[pl.BlockSpec(memory_space=pltpu.SMEM)] * 2 + [whole] * 3,
        out_specs=(whole, whole),
        scratch_shapes=[
            pltpu.VMEM((levels, size_x, size_y + 16, members), f32),
            pltpu.VMEM((2, levels, size_x, members), f32),
            pltpu.VMEM((2, levels, size_y, members), f32),
            pltpu.VMEM((2, levels, size_x, members), f32),
            pltpu.VMEM((sections, nty, 2, rows, lanes), f32),
            [pltpu.VMEM((nty, 2, rows, lanes), f32)] * sections,
            pltpu.VMEM((sections, ntx, share, rows, lanes), f32),
            pltpu.VMEM((sections, ntx, share, rows, lanes), f32),
            dma((4,)), dma((4,)),
            dma((sections, nty)), dma((sections, nty)), dma((sections, ntx)), dma((sections, ntx)),
            dma((sections, nty)), dma((sections, nty)), dma((sections, ntx)), dma((sections, ntx)),
        ],
        compiler_params=pltpu.CompilerParams(
            collective_id=0, has_side_effects=True, vmem_limit_bytes=32 * 2**20),
    )(owner_tiles // nty, owner_tiles % nty, prior_state, speeds, my_cells)


def terms(a):
    high = a.astype(jnp.bfloat16)
    return high, (a - high.astype(jnp.float32)).astype(jnp.bfloat16)


def update_kernel(chunk, reach_x, reach_y, state_ref, slots_ref, noise_ref, line_ref, own_ref, out_ref,
                  column_ref, all_ref, anom_ref, innov_ref):
    sections, ntx, nty, share, rows, lanes = slots_ref.shape
    cells, members = state_ref.shape
    observed = noise_ref.shape[1]
    per = nty * rows
    for s in range(sections):
        for h in range(2 * observed // per):
            all_ref[pl.ds(s * observed + h // 2 * per, per), pl.ds(h % 2 * lanes, lanes)] = slots_ref[
                s, h // share, :, h % share].reshape(per, lanes)
    total = sections * observed + cells
    all_ref[pl.ds(sections * observed, cells), :] = state_ref[...]
    for s in range(sections):
        column_ref[pl.ds(s * observed, observed), :] = line_ref[s].T
    column_ref[pl.ds(sections * observed, cells), :] = own_ref[...].T
    for s in range(sections):
        start = s * observed
        prior_obs = all_ref[pl.ds(start, observed), :]
        anomaly = prior_obs - jnp.mean(prior_obs, axis=1, keepdims=True)
        value = column_ref[pl.ds(start, observed), 3:4]
        error = column_ref[pl.ds(start, observed), 4:5]
        factor = 1.0 / (jnp.sum(anomaly * anomaly, axis=1, keepdims=True) + (members - 1) * error)
        innovation = (value + jnp.sqrt(error) * noise_ref[s] - prior_obs) * factor
        high, low = terms(anomaly)
        anom_ref[...] = jnp.concatenate([high, high, low], axis=1)
        high, low = terms(innovation)
        innov_ref[...] = jnp.concatenate([high, high, low], axis=0)
        level_o = line_ref[s, 0:1, :]
        x_o = line_ref[s, 1:2, :]
        y_o = line_ref[s, 2:3, :]

        def refresh(at):
            block = all_ref[pl.ds(at, chunk), :]
            level = column_ref[pl.ds(at, chunk), 0:1]
            x = column_ref[pl.ds(at, chunk), 1:2]
            y = column_ref[pl.ds(at, chunk), 2:3]
            high, low = terms(block - jnp.mean(block, axis=1, keepdims=True))
            covar = lax.dot_general(
                jnp.concatenate([high, low, high], axis=1), anom_ref[...], (((1,), (1,)), ((), ())),
                preferred_element_type=jnp.float32)
            near_x = jnp.maximum(0.0, 1.0 - jnp.abs(x - x_o) * (1.0 / reach_x))
            near_y = jnp.maximum(0.0, 1.0 - jnp.abs(y - y_o) * (1.0 / reach_y))
            near = near_x * near_y
            weights = covar * (near * near * jnp.where(level == level_o, 1.0, VERT_COEF))
            high, low = terms(weights)
            return block + jnp.dot(
                jnp.concatenate([high, low, high], axis=1), innov_ref[...], preferred_element_type=jnp.float32)

        first = start + observed
        if s + 1 < sections:
            for n in range((total - first) // chunk):
                at = first + n * chunk
                all_ref[pl.ds(at, chunk), :] = refresh(at)
        else:
            for n in range(cells // chunk):
                out_ref[pl.ds(n * chunk, chunk), :] = refresh(first + n * chunk)


def update(state, slots, noise, line, own, reach_x, reach_y):
    sections, observed, members = noise.shape
    cells = state.shape[0]
    total = sections * observed + cells
    chunk = 256
    whole = pl.BlockSpec(memory_space=pltpu.VMEM)
    return pl.pallas_call(
        functools.partial(update_kernel, chunk, reach_x, reach_y),
        out_shape=jax.ShapeDtypeStruct((cells, members), jnp.float32),
        in_specs=[whole] * 5,
        out_specs=whole,
        scratch_shapes=[
            pltpu.VMEM((total, 8), jnp.float32),
            pltpu.VMEM((total, members), jnp.float32),
            pltpu.VMEM((observed, 3 * members), jnp.bfloat16),
            pltpu.VMEM((3 * observed, members), jnp.bfloat16),
        ],
        compiler_params=pltpu.CompilerParams(vmem_limit_bytes=48 * 2**20),
    )(state, slots, noise, line, own)


def on_device(
    prior_state, east_vel, north_vel, owner_tiles, obs_cells, obs_value, obs_error, obs_pert
):
    levels, size_x, size_y, members = prior_state.shape
    section_count, owner_count, obs_count = obs_cells.shape
    ntx, nty = lax.axis_size("tx"), lax.axis_size("ty")
    column_idx = lax.axis_index("tx")
    row_idx = lax.axis_index("ty")
    my_tile = column_idx * nty + row_idx
    cells = levels * size_x * size_y

    mine = owner_tiles == my_tile
    my_cells = jnp.sum(jnp.where(mine[:, :, None], obs_cells, 0), axis=1)
    speeds = jnp.stack([east_vel.reshape(cells), north_vel.reshape(cells)], axis=1)
    state, slots = spread(prior_state, speeds, my_cells.reshape(-1, 1), owner_tiles, ntx, nty)

    level_o, x_o, y_o = positions(owner_tiles[:, :, None], obs_cells, size_x, size_y, nty)
    own = jnp.arange(cells, dtype=jnp.int32)
    level_c = own // (size_x * size_y)
    x_c = column_idx * size_x + own % (size_x * size_y) // size_y
    y_c = row_idx * size_y + own % size_y
    rows_of = lambda parts: jnp.stack([a.astype(jnp.float32) for a in parts + parts[:8 - len(parts)]], axis=-2)
    line = rows_of([a.reshape(section_count, -1) for a in (level_o, x_o, y_o, obs_value, obs_error)])
    own = rows_of([level_c, x_c, y_c, x_c, y_c])
    noise = obs_pert.reshape(section_count, owner_count * obs_count, members)
    out = update(state, slots, noise, line, own, 3.0 * size_x, 3.0 * size_y)
    return out.reshape(levels, size_x, size_y, members)


def solution(mesh):
    placed = (
        P(None, "tx", "ty", None),
        P(None, "tx", "ty"),
        P(None, "tx", "ty"),
        P(),
        P(),
        P(),
        P(),
        P(),
    )
    return jax.shard_map(
        on_device, mesh=mesh, in_specs=placed, out_specs=P(None, "tx", "ty", None), check_vma=False
    )
```
